512 devices in a mesh: fsdp: 32 (over y_hi, x, core), tensor: 16 (over y_lo, z).
Axes of the slice: x: 4, y: 8 (y_hi: 4, y_lo: 2; y = y_hi * 2 + y_lo), z: 8, core: 2. Of those that a mesh axis runs over, the one named last changes fastest.
Arguments:
- moment: bfloat16 [4096, 12800], P('fsdp', 'tensor'), may hold values from -4.5 to 4.5
Outputs:
- updated: bfloat16 [4096, 12800], P('fsdp', 'tensor')
The draws below stay inside these ranges and needn't reach their ends.
All inputs are finite; a program needn't handle non-finite values.
Results may differ from the reference program's by a relative error of at most 0.0097.
Values may be sent and summed in bfloat16 or wider, within the bound.
No kernel may reach another device: no remote copies, remote signals or barrier semaphores. Data moves between devices by JAX's collectives and lax.ppermute only.
A program may use at most 64 MiB of HBM per device.

```python
import jax
import jax.numpy as jnp
from jax import lax

ROWS = 4096
COLS = 12800


def draw_moment(key, part):
    key = jax.random.fold_in(key, 11)
    values = jax.random.normal(key, (ROWS, COLS), jnp.float32)
    return jnp.clip(values, -4.5, 4.5).astype(jnp.bfloat16)


def setup_inputs(seed: int = 0) -> dict:
    keys = jax.random.split(jax.random.key(seed), 2)
    return {
        "moment": draw_moment(jax.random.fold_in(keys[1], 71), 0),
    }


coef_linear = 3.4445
coef_cubic = -4.7750
coef_quintic = 2.0315


def reference(moment):
    wide = moment.astype(jnp.float32)
    highest = lax.Precision.HIGHEST
    gram = (jnp.dot(wide, wide.T, precision=highest) / COLS).astype(jnp.bfloat16)
    gram_wide = gram.astype(jnp.float32)
    first = jnp.dot(gram_wide, wide, precision=highest).astype(jnp.bfloat16)
    second = jnp.dot(gram_wide, first.astype(jnp.float32), precision=highest)
    updated = coef_linear * wide + coef_cubic * first.astype(jnp.float32) + coef_quintic * second
    return updated.astype(jnp.bfloat16)
```

```python
import jax
import jax.numpy as jnp
import numpy as np
from jax import lax
from jax.sharding import Mesh, PartitionSpec as P

COLS = 12800

coef_linear = 3.4445
coef_cubic = -4.775
coef_quintic = 2.0315

SPLIT = {"yh": 4, "x": 4, "core": 2, "yl": 2, "zh": 4, "zl": 2}
PAIRS = ("yl", "zl")
SUM_GROUP = PAIRS + ("zh",)
SWAP = [(0, 1), (1, 0)]


def spread(block, axes):
    return lax.all_to_all(jnp.broadcast_to(block[None], (4,) + block.shape), axes, 0, 0)


def collect(parts, own, axis):
    others = lax.all_to_all(parts, axis, 0, 0)
    index = lax.broadcasted_iota(jnp.int32, others.shape, 0)
    others = jnp.where(index == lax.axis_index(axis), 0.0, others.astype(jnp.float32))
    return own + jnp.sum(others, axis=0)


def both_cores(blocks):
    return jnp.stack([blocks, lax.ppermute(blocks, "core", SWAP)], axis=1)


def on_device(moment):
    mine = moment.T
    along, across = spread(mine, "x"), lax.all_gather(mine, "yh")
    along, across = lax.optimization_barrier((along, across))
    across = both_cores(across)

    gram = jnp.einsum("ecs,dfct->edsft", along, across, preferred_element_type=jnp.float32)
    gram = (gram / COLS).astype(jnp.bfloat16).reshape(16, *gram.shape[2:])
    gram = lax.all_to_all(gram, SUM_GROUP, 0, 0)
    gram = lax.reduce_precision(jnp.sum(gram.astype(jnp.float32), axis=0), 8, 7)
    gram = spread(lax.all_gather(gram.astype(jnp.bfloat16), "zh"), PAIRS)
    mine_only = lax.dynamic_slice_in_dim(gram, lax.axis_index("x"), 1, 0)

    def product(columns):
        def part(rows):
            return jnp.einsum("dfct,edsft->ecs", columns, rows, preferred_element_type=jnp.float32)

        return collect(part(gram).astype(jnp.bfloat16), part(mine_only)[0], "x")

    first = lax.reduce_precision(product(across), 8, 7)
    second = product(both_cores(lax.all_gather(first.astype(jnp.bfloat16), "yh")))

    updated = coef_linear * mine.astype(jnp.float32) + coef_cubic * first + coef_quintic * second
    return updated.astype(jnp.bfloat16).T


def solution(mesh):
    devices = np.asarray(mesh.devices).reshape(tuple(SPLIT.values()))
    fine = Mesh(devices, tuple(SPLIT))
    spec = P(("yh", "x", "core"), ("yl", "zh", "zl"))
    return jax.shard_map(on_device, mesh=fine, in_specs=(spec,), out_specs=spec, check_vma=False)
```

```python
import jax
import jax.numpy as jnp
import numpy as np
from jax import lax
from jax.sharding import Mesh, PartitionSpec as P

COLS = 12800

coef_linear = 3.4445
coef_cubic = -4.775
coef_quintic = 2.0315

SPLIT = {"yh": 4, "x": 4, "core": 2, "yl": 2, "zh": 4, "zl": 2}
PAIRS = ("yl", "zl")
SWAP = [(0, 1), (1, 0)]


def spread(block, axes):
    return lax.all_to_all(jnp.broadcast_to(block[None], (4,) + block.shape), axes, 0, 0)


def collect(parts, own, axis):
    others = lax.all_to_all(parts, axis, 0, 0)
    index = lax.broadcasted_iota(jnp.int32, others.shape, 0)
    others = jnp.where(index == lax.axis_index(axis), 0.0, others.astype(jnp.float32))
    return own + jnp.sum(others, axis=0)


def total(parts):
    return lax.reduce_precision(jnp.sum(parts.astype(jnp.float32), axis=0), 8, 7).astype(jnp.bfloat16)


def both_cores(blocks):
    return jnp.stack([blocks, lax.ppermute(blocks, "core", SWAP)], axis=1)


def on_device(moment):
    mine = moment.T
    along, across = spread(mine, "x"), lax.all_gather(mine, "yh")
    along, across = lax.optimization_barrier((along, across))
    across = both_cores(across)

    gram = jnp.einsum("ecs,dfct->edsft", along, across, preferred_element_type=jnp.float32)
    gram = lax.all_to_all((gram / COLS).astype(jnp.bfloat16), PAIRS, 0, 0)
    gram = total(lax.all_to_all(total(gram), "zh", 0, 0))
    gram = spread(spread(gram, "zh"), PAIRS)
    mine_only = lax.dynamic_slice_in_dim(gram, lax.axis_index("x"), 1, 0)

    def product(columns):
        def part(rows):
            return jnp.einsum("dfct,edsft->ecs", columns, rows, preferred_element_type=jnp.float32)

        return collect(part(gram).astype(jnp.bfloat16), part(mine_only)[0], "x")

    first = lax.reduce_precision(product(across), 8, 7)
    second = product(both_cores(lax.all_gather(first.astype(jnp.bfloat16), "yh")))

    updated = coef_linear * mine.astype(jnp.float32) + coef_cubic * first + coef_quintic * second
    return updated.astype(jnp.bfloat16).T


def solution(mesh):
    devices = np.asarray(mesh.devices).reshape(tuple(SPLIT.values()))
    fine = Mesh(devices, tuple(SPLIT))
    spec = P(("yh", "x", "core"), ("yl", "zh", "zl"))
    return jax.shard_map(on_device, mesh=fine, in_specs=(spec,), out_specs=spec, check_vma=False)
```

```python
import jax
import jax.numpy as jnp
import numpy as np
from jax import lax
from jax.sharding import Mesh, PartitionSpec as P

COLS = 12800

coef_linear = 3.4445
coef_cubic = -4.775
coef_quintic = 2.0315

SPLIT = {"yh": 4, "x": 4, "core": 2, "yl": 2, "zh": 4, "zl": 2}
PAIRS = ("yl", "zl")
SWAP = [(0, 1), (1, 0)]


def spread(block, axes):
    return lax.all_to_all(jnp.broadcast_to(block[None], (4,) + block.shape), axes, 0, 0)


def others(parts, axis):
    parts = lax.all_to_all(parts, axis, 0, 0)
    index = lax.broadcasted_iota(jnp.int32, parts.shape, 0)
    parts = jnp.where(index == lax.axis_index(axis), 0.0, parts.astype(jnp.float32))
    return jnp.sum(parts, axis=0)


def total(parts):
    return lax.reduce_precision(jnp.sum(parts.astype(jnp.float32), axis=0), 8, 7).astype(jnp.bfloat16)


def both_cores(blocks):
    return jnp.stack([blocks, lax.ppermute(blocks, "core", SWAP)], axis=1)


def on_device(moment):
    mine = moment.T
    along, across = spread(mine, "x"), lax.all_gather(mine, "yh")
    along, across = lax.optimization_barrier((along, across))
    across = both_cores(across)

    gram = jnp.einsum("ecs,dfct->edsft", along, across, preferred_element_type=jnp.float32)
    gram = lax.all_to_all((gram / COLS).astype(jnp.bfloat16), PAIRS, 0, 0)
    gram = total(lax.all_to_all(total(gram), "zh", 0, 0))
    gram = spread(spread(gram, "zh"), PAIRS)
    mine_only = lax.dynamic_slice_in_dim(gram, lax.axis_index("x"), 1, 0)

    def product(columns):
        def part(rows):
            return jnp.einsum("dfct,edsft->ecs", columns, rows, preferred_element_type=jnp.float32)

        return part(gram).astype(jnp.bfloat16), part(mine_only)[0]

    parts, own = product(across)
    own = lax.optimization_barrier(own)
    first = lax.reduce_precision(own + others(parts, "x"), 8, 7)
    parts, own = product(both_cores(lax.all_gather(first.astype(jnp.bfloat16), "yh")))
    known = coef_linear * mine.astype(jnp.float32) + coef_cubic * first + coef_quintic * own
    known = lax.optimization_barrier(known)
    updated = known + coef_quintic * others(parts, "x")
    return updated.astype(jnp.bfloat16).T


def solution(mesh):
    devices = np.asarray(mesh.devices).reshape(tuple(SPLIT.values()))
    fine = Mesh(devices, tuple(SPLIT))
    spec = P(("yh", "x", "core"), ("yl", "zh", "zl"))
    return jax.shard_map(on_device, mesh=fine, in_specs=(spec,), out_specs=spec, check_vma=False)
```

```python
import jax
import jax.numpy as jnp
import numpy as np
from jax import lax
from jax.sharding import Mesh, PartitionSpec as P

COLS = 12800

coef_linear = 3.4445
coef_cubic = -4.775
coef_quintic = 2.0315

SPLIT = {"yh": 4, "x": 4, "core": 2, "yl": 2, "zh": 4, "zl": 2}
PAIRS = ("yl", "zl")
SWAP = [(0, 1), (1, 0)]


def spread(block, axes):
    return lax.all_to_all(jnp.broadcast_to(block[None], (4,) + block.shape), axes, 0, 0)


def others(parts, axis):
    parts = lax.all_to_all(parts, axis, 0, 0)
    index = lax.broadcasted_iota(jnp.int32, parts.shape, 0)
    parts = jnp.where(index == lax.axis_index(axis), 0.0, parts.astype(jnp.float32))
    return jnp.sum(parts, axis=0)


def total(parts):
    return lax.reduce_precision(jnp.sum(parts.astype(jnp.float32), axis=0), 8, 7).astype(jnp.bfloat16)


def both_cores(blocks):
    return jnp.stack([blocks, lax.ppermute(blocks, "core", SWAP)], axis=1)


def on_device(moment):
    mine = moment.T
    along, across = spread(mine, "x"), lax.all_gather(mine, "yh")
    along, across = lax.optimization_barrier((along, across))
    across = both_cores(across)

    gram = jnp.einsum("ecs,dfct->edsft", along, across, preferred_element_type=jnp.float32)
    gram = lax.all_to_all((gram / COLS).astype(jnp.bfloat16), PAIRS, 0, 0)
    gram = total(lax.all_to_all(total(gram), "zh", 0, 0))
    gram = spread(spread(gram, "zh"), PAIRS)
    mine_only = lax.dynamic_slice_in_dim(gram, lax.axis_index("x"), 1, 0)

    def product(columns):
        def part(rows):
            return jnp.einsum("dfct,edsft->ecs", columns, rows, preferred_element_type=jnp.float32)

        return part(gram).astype(jnp.bfloat16), part(mine_only)[0]

    parts, own = product(across)
    own = lax.optimization_barrier(own)
    first = lax.reduce_precision(own + others(parts, "x"), 8, 7)
    parts, own = product(both_cores(lax.all_gather(first.astype(jnp.bfloat16), "yh")))
    second = own + others(parts, "x")

    updated = coef_linear * mine.astype(jnp.float32) + coef_cubic * first + coef_quintic * second
    return updated.astype(jnp.bfloat16).T


def solution(mesh):
    devices = np.asarray(mesh.devices).reshape(tuple(SPLIT.values()))
    fine = Mesh(devices, tuple(SPLIT))
    spec = P(("yh", "x", "core"), ("yl", "zh", "zl"))
    return jax.shard_map(on_device, mesh=fine, in_specs=(spec,), out_specs=spec, check_vma=False)
```

```python
import jax
import jax.numpy as jnp
import numpy as np
from jax import lax
from jax.sharding import Mesh, PartitionSpec as P

COLS = 12800

coef_linear = 3.4445
coef_cubic = -4.775
coef_quintic = 2.0315

SPLIT = {"yh": 4, "x": 4, "core": 2, "yl": 2, "zh": 4, "zl": 2}
PAIRS = ("yl", "zl")
SWAP = [(0, 1), (1, 0)]


def spread(block, axes):
    return lax.all_to_all(jnp.broadcast_to(block[None], (4,) + block.shape), axes, 0, 0)


def others(parts, axis):
    parts = lax.all_to_all(parts, axis, 0, 0)
    index = lax.broadcasted_iota(jnp.int32, parts.shape, 0)
    parts = jnp.where(index == lax.axis_index(axis), 0.0, parts.astype(jnp.float32))
    return jnp.sum(parts, axis=0)


def total(parts):
    return lax.reduce_precision(jnp.sum(parts.astype(jnp.float32), axis=0), 8, 7).astype(jnp.bfloat16)


def both_cores(blocks):
    return jnp.stack([blocks, lax.ppermute(blocks, "core", SWAP)], axis=1)


def on_device(moment):
    mine = moment.T
    along, across = spread(mine, "x"), lax.all_gather(mine, "yh")
    along, across = lax.optimization_barrier((along, across))
    across = both_cores(across)

    gram = jnp.einsum("ecs,dfct->edsft", along, across, preferred_element_type=jnp.float32)
    gram = lax.all_to_all((gram / COLS).astype(jnp.bfloat16), PAIRS, 0, 0)
    gram = total(lax.all_to_all(total(gram), "zh", 0, 0))
    gram = spread(lax.all_gather(gram, "zh"), PAIRS)
    mine_only = lax.dynamic_slice_in_dim(gram, lax.axis_index("x"), 1, 0)

    def product(columns):
        def part(rows):
            return jnp.einsum("dfct,edsft->ecs", columns, rows, preferred_element_type=jnp.float32)

        return part(gram).astype(jnp.bfloat16), part(mine_only)[0]

    parts, own = product(across)
    own = lax.optimization_barrier(own)
    first = lax.reduce_precision(own + others(parts, "x"), 8, 7)
    parts, own = product(both_cores(lax.all_gather(first.astype(jnp.bfloat16), "yh")))
    second = own + others(parts, "x")

    updated = coef_linear * mine.astype(jnp.float32) + coef_cubic * first + coef_quintic * second
    return updated.astype(jnp.bfloat16).T


def solution(mesh):
    devices = np.asarray(mesh.devices).reshape(tuple(SPLIT.values()))
    fine = Mesh(devices, tuple(SPLIT))
    spec = P(("yh", "x", "core"), ("yl", "zh", "zl"))
    return jax.shard_map(on_device, mesh=fine, in_specs=(spec,), out_specs=spec, check_vma=False)
```

```python
import jax
import jax.numpy as jnp
import numpy as np
from jax import lax
from jax.sharding import Mesh, PartitionSpec as P

COLS = 12800

coef_linear = 3.4445
coef_cubic = -4.775
coef_quintic = 2.0315

SPLIT = {"yh": 4, "x": 4, "core": 2, "yl": 2, "zh": 4, "zl": 2}
PAIRS = ("zl", "yl")
SWAP = [(0, 1), (1, 0)]


def spread(block, axes):
    return lax.all_to_all(jnp.broadcast_to(block[None], (4,) + block.shape), axes, 0, 0)


def others(parts, axis):
    parts = lax.all_to_all(parts, axis, 0, 0)
    index = lax.broadcasted_iota(jnp.int32, parts.shape, 0)
    parts = jnp.where(index == lax.axis_index(axis), 0.0, parts.astype(jnp.float32))
    return jnp.sum(parts, axis=0)


def total(parts):
    return lax.reduce_precision(jnp.sum(parts.astype(jnp.float32), axis=0), 8, 7).astype(jnp.bfloat16)


def both_cores(blocks):
    return jnp.stack([blocks, lax.ppermute(blocks, "core", SWAP)], axis=1)


def on_device(moment):
    mine = moment.T
    along, across = spread(mine, "x"), lax.all_gather(mine, "yh")
    along, across = lax.optimization_barrier((along, across))
    across = both_cores(across)

    gram = jnp.einsum("ecs,dfct->edsft", along, across, preferred_element_type=jnp.float32)
    gram = lax.all_to_all((gram / COLS).astype(jnp.bfloat16), PAIRS, 0, 0)
    gram = total(lax.all_to_all(total(gram), "zh", 0, 0))
    gram = spread(spread(gram, "zh"), PAIRS)
    mine_only = lax.dynamic_slice_in_dim(gram, lax.axis_index("x"), 1, 0)

    def product(columns):
        def part(rows):
            return jnp.einsum("dfct,edsft->ecs", columns, rows, preferred_element_type=jnp.float32)

        return part(gram).astype(jnp.bfloat16), part(mine_only)[0]

    parts, own = product(across)
    own = lax.optimization_barrier(own)
    first = lax.reduce_precision(own + others(parts, "x"), 8, 7)
    parts, own = product(both_cores(lax.all_gather(first.astype(jnp.bfloat16), "yh")))
    second = own + others(parts, "x")

    updated = coef_linear * mine.astype(jnp.float32) + coef_cubic * first + coef_quintic * second
    return updated.astype(jnp.bfloat16).T


def solution(mesh):
    devices = np.asarray(mesh.devices).reshape(tuple(SPLIT.values()))
    fine = Mesh(devices, tuple(SPLIT))
    spec = P(("yh", "x", "core"), ("yl", "zh", "zl"))
    return jax.shard_map(on_device, mesh=fine, in_specs=(spec,), out_specs=spec, check_vma=False)
```

```python
import jax
import jax.numpy as jnp
import numpy as np
from jax import lax
from jax.sharding import Mesh, PartitionSpec as P

COLS = 12800

coef_linear = 3.4445
coef_cubic = -4.775
coef_quintic = 2.0315

SPLIT = {"yh": 4, "x": 4, "core": 2, "yl": 2, "zh": 4, "zl": 2}
PAIRS = ("yl", "zl")
SWAP = [(0, 1), (1, 0)]


def spread(block, axes):
    return lax.all_to_all(jnp.broadcast_to(block[None], (4,) + block.shape), axes, 0, 0)


def others(parts, axis):
    parts = lax.all_to_all(parts, axis, 0, 0)
    index = lax.broadcasted_iota(jnp.int32, parts.shape, 0)
    parts = jnp.where(index == lax.axis_index(axis), 0.0, parts.astype(jnp.float32))
    return jnp.sum(parts, axis=0)


def total(parts):
    return lax.reduce_precision(jnp.sum(parts.astype(jnp.float32), axis=0), 8, 7).astype(jnp.bfloat16)


def both_cores(blocks):
    return jnp.stack([blocks, lax.ppermute(blocks, "core", SWAP)], axis=1)


def on_device(moment):
    mine = moment.T
    along, across = spread(mine, "x"), lax.all_gather(mine, "yh")
    along, across = lax.optimization_barrier((along, across))
    across = both_cores(across)

    gram = jnp.einsum("ecs,dfct->edsft", along, across, preferred_element_type=jnp.float32)
    gram = lax.all_to_all((gram / COLS).astype(jnp.bfloat16), PAIRS, 0, 0)
    gram = total(lax.all_to_all(total(gram), "zh", 0, 0))
    gram = spread(spread(gram, "zh"), PAIRS)
    mine_only = lax.dynamic_slice_in_dim(gram, lax.axis_index("x"), 1, 0)

    def product(columns):
        def part(rows):
            return jnp.einsum("dfct,edsft->ecs", columns, rows, preferred_element_type=jnp.float32)

        return part(gram).astype(jnp.bfloat16), part(mine_only)[0]

    parts, own = product(across)
    own = lax.optimization_barrier(own)
    first = lax.reduce_precision(own + others(parts, "x"), 8, 7)
    blocks = lax.all_gather(first.astype(jnp.bfloat16), "yh")
    known = coef_linear * mine.astype(jnp.float32) + coef_cubic * first
    partner, known = lax.optimization_barrier((lax.ppermute(blocks, "core", SWAP), known))
    parts, own = product(jnp.stack([blocks, partner], axis=1))
    updated = known + coef_quintic * (own + others(parts, "x"))
    return updated.astype(jnp.bfloat16).T


def solution(mesh):
    devices = np.asarray(mesh.devices).reshape(tuple(SPLIT.values()))
    fine = Mesh(devices, tuple(SPLIT))
    spec = P(("yh", "x", "core"), ("yl", "zh", "zl"))
    return jax.shard_map(on_device, mesh=fine, in_specs=(spec,), out_specs=spec, check_vma=False)
```

```python
import jax
import jax.numpy as jnp
import numpy as np
from jax import lax
from jax.sharding import Mesh, PartitionSpec as P

COLS = 12800

coef_linear = 3.4445
coef_cubic = -4.775
coef_quintic = 2.0315

SPLIT = {"yh": 4, "x": 4, "core": 2, "yl": 2, "zh": 4, "zl": 2}
PAIRS = ("yl", "zl")
SWAP = [(0, 1), (1, 0)]


def spread(block, axes):
    return lax.all_to_all(jnp.broadcast_to(block[None], (4,) + block.shape), axes, 0, 0)


def others(parts, axis):
    parts = lax.all_to_all(parts, axis, 0, 0)
    index = lax.broadcasted_iota(jnp.int32, parts.shape, 0)
    parts = jnp.where(index == lax.axis_index(axis), 0.0, parts.astype(jnp.float32))
    return jnp.sum(parts, axis=0)


def total(parts):
    return lax.reduce_precision(jnp.sum(parts.astype(jnp.float32), axis=0), 8, 7).astype(jnp.bfloat16)


def both_cores(blocks):
    return jnp.stack([blocks, lax.ppermute(blocks, "core", SWAP)], axis=1)


def on_device(moment):
    mine = moment.T
    along, across = spread(mine, "x"), lax.all_gather(mine, "yh")
    along, across = lax.optimization_barrier((along, across))
    across = both_cores(across)

    gram = jnp.einsum("ecs,dfct->edsft", along, across, preferred_element_type=jnp.float32)
    gram = lax.all_to_all((gram / COLS).astype(jnp.bfloat16), PAIRS, 0, 0)
    gram = total(lax.all_to_all(total(gram), "zh", 0, 0))
    gram = spread(spread(gram, "zh"), PAIRS)
    mine_only = lax.dynamic_slice_in_dim(gram, lax.axis_index("x"), 1, 0)

    def product(columns):
        def part(rows):
            return jnp.einsum("dfct,edsft->ecs", columns, rows, preferred_element_type=jnp.float32)

        return part(gram).astype(jnp.bfloat16), part(mine_only)[0]

    parts, own = product(across)
    own = lax.optimization_barrier(own)
    first = lax.reduce_precision(own + others(parts, "x"), 8, 7)
    blocks = lax.all_gather(first.astype(jnp.bfloat16), "yh")
    known = coef_linear * mine.astype(jnp.float32) + coef_cubic * first
    def share(columns, f, rows):
        return jnp.einsum(
            "dct,edst->ecs", columns, rows[:, :, :, f], preferred_element_type=jnp.float32
        )

    partner = lax.ppermute(blocks, "core", SWAP)
    near, near_own = share(blocks, 0, gram), share(blocks, 0, mine_only)[0]
    known = known + coef_quintic * near_own
    partner, near, known = lax.optimization_barrier((partner, near, known))
    parts = (near + share(partner, 1, gram)).astype(jnp.bfloat16)
    own = share(partner, 1, mine_only)[0]
    updated = known + coef_quintic * (own + others(parts, "x"))
    return updated.astype(jnp.bfloat16).T


def solution(mesh):
    devices = np.asarray(mesh.devices).reshape(tuple(SPLIT.values()))
    fine = Mesh(devices, tuple(SPLIT))
    spec = P(("yh", "x", "core"), ("yl", "zh", "zl"))
    return jax.shard_map(on_device, mesh=fine, in_specs=(spec,), out_specs=spec, check_vma=False)
```

```python
import jax
import jax.numpy as jnp
import numpy as np
from jax import lax
from jax.sharding import Mesh, PartitionSpec as P

COLS = 12800

coef_linear = 3.4445
coef_cubic = -4.775
coef_quintic = 2.0315

SPLIT = {"yh": 4, "x": 4, "core": 2, "yl": 2, "zh": 4, "zl": 2}
PAIRS = ("zl", "yl")
SWAP = [(0, 1), (1, 0)]


def spread(block, axes):
    return lax.all_to_all(jnp.broadcast_to(block[None], (4,) + block.shape), axes, 0, 0)


def others(parts, axis):
    parts = lax.all_to_all(parts, axis, 0, 0)
    index = lax.broadcasted_iota(jnp.int32, parts.shape, 0)
    parts = jnp.where(index == lax.axis_index(axis), 0.0, parts.astype(jnp.float32))
    return jnp.sum(parts, axis=0)


def total(parts):
    return lax.reduce_precision(jnp.sum(parts.astype(jnp.float32), axis=0), 8, 7).astype(jnp.bfloat16)


def both_cores(blocks):
    return jnp.stack([blocks, lax.ppermute(blocks, "core", SWAP)], axis=1)


def on_device(moment):
    mine = moment.T
    along, across = spread(mine, "x"), lax.all_gather(mine, "yh")
    along, across = lax.optimization_barrier((along, across))
    across = both_cores(across)

    gram = jnp.einsum("ecs,dfct->edsft", along, across, preferred_element_type=jnp.float32)
    gram = lax.all_to_all((gram / COLS).astype(jnp.bfloat16), PAIRS, 0, 0)
    gram = total(lax.all_to_all(total(gram), "zh", 0, 0))
    gram = spread(spread(gram, "zh"), PAIRS)
    mine_only = lax.dynamic_slice_in_dim(gram, lax.axis_index("x"), 1, 0)

    def product(columns):
        def part(rows):
            return jnp.einsum("dfct,edsft->ecs", columns, rows, preferred_element_type=jnp.float32)

        return part(gram).astype(jnp.bfloat16), part(mine_only)[0]

    parts, own = product(across)
    own = lax.optimization_barrier(own)
    first = lax.reduce_precision(own + others(parts, "x"), 8, 7)
    blocks = lax.all_gather(first.astype(jnp.bfloat16), "yh")
    known = coef_linear * mine.astype(jnp.float32) + coef_cubic * first
    partner, known = lax.optimization_barrier((lax.ppermute(blocks, "core", SWAP), known))
    parts, own = product(jnp.stack([blocks, partner], axis=1))
    updated = known + coef_quintic * (own + others(parts, "x"))
    return updated.astype(jnp.bfloat16).T


def solution(mesh):
    devices = np.asarray(mesh.devices).reshape(tuple(SPLIT.values()))
    fine = Mesh(devices, tuple(SPLIT))
    spec = P(("yh", "x", "core"), ("yl", "zh", "zl"))
    return jax.shard_map(on_device, mesh=fine, in_specs=(spec,), out_specs=spec, check_vma=False)
```
